256 devices in a mesh: expert: 32 (over y, z_hi, core), cuts: 8 (over z_lo, x).
Axes of the slice: x: 4, y: 4, z: 8 (z_hi: 4, z_lo: 2; z = z_hi * 2 + z_lo), core: 2. Of those that a mesh axis runs over, the one named last changes fastest.
Arguments:
- tokens: bfloat16 [4096, 3584], P('expert', 'cuts'), may hold values from -6 to 6
- routing: int32 [4096, 8], P('expert'), may hold values from 0 to 31, all different within a row; in each aligned block of 128 rows (0 to 127, 128 to 255, ...) at most 40 rows name the same one
- gate_weights: float32 [4096, 8], P('expert'), may hold values from 0.05 to 0.6
- owner: int32 [32], replicated, may hold values from 0 to 31, each once
- weights: bfloat16 [32, 2, 3584, 1024], P('expert', None, None, 'cuts'), may hold values from -0.09375 to 0.09375
- grads: bfloat16 [32, 2, 3584, 1024], P('expert', None, None, 'cuts'), may hold values from -6 to 6
- first: bfloat16 [32, 2, 3584, 1024], P('expert', None, None, 'cuts'), may hold values from -4 to 4
- second: bfloat16 [32, 2, 3584, 1024], P('expert', None, None, 'cuts'), may hold values from 0.049804688 to 2
Outputs:
- mixed: bfloat16 [4096, 3584], P('expert', 'cuts')
- new_weights: bfloat16 [32, 2, 3584, 1024], P('expert', None, None, 'cuts')
- new_first: bfloat16 [32, 2, 3584, 1024], P('expert', None, None, 'cuts')
- new_second: bfloat16 [32, 2, 3584, 1024], P('expert', None, None, 'cuts')
The draws below stay inside these ranges and needn't reach their ends.
Inputs may be any that keep to these rules, and one draw needn't show every extreme that they name: `routing`: each row names 8 different experts; among the 128 rows of one device no expert is named more than 40 times, and in every draw some expert is named exactly 40 times there. A permutation: expert e, held at index e of the expert axis before migration, is held at index owner[e] after it.
All inputs are finite; a program needn't handle non-finite values.
Results may differ from the reference program's by a relative error of at most 0.015.
Values may be sent and summed in bfloat16 or wider, within the bound.
No kernel may reach another device: no remote copies, remote signals or barrier semaphores. Data moves between devices by JAX's collectives and lax.ppermute only.
A program may use at most 128 MiB of HBM per device.

```python
import math
import jax
import jax.numpy as jnp
import numpy as np
from jax import lax

D = 3584
FF = 1024
TOPK = 8
TOK_DEV = 128
EXPERTS = 32
TOKENS = 4096
CAP = 40
FF_GROUP = 128
N_EXPERT = 32
N_CUTS = 8


def block_levels(stream_key, dims, pieces, smallest, largest):
    loudness, own = 1.0, jax.random.fold_in(stream_key, 6)
    for position, parts in pieces:
        draws = jnp.exp(jax.random.uniform(jax.random.fold_in(own, position), (parts,), jnp.float32, smallest / len(pieces), largest / len(pieces)))
        loudness = loudness * jnp.repeat(draws, dims[position] // parts).reshape([-1 if axis == position else 1 for axis in range(len(dims))])
    return loudness


def deal_out(key, own, number, rows, count, top, limit, lean):
    order = jax.random.permutation(key, count)
    crowded, common = portions_of(count, rows * top, limit, lean, True), portions_of(count, rows * top, limit, lean, False)
    places = jnp.arange(count)

    def named(sizes, rotation):
        used = int((sizes > 0).sum())
        fixed = max(1, used // 4)
        passed = fixed + (places - fixed + rotation * (used - fixed)) % max(1, count - fixed)
        return jnp.zeros((count,), jnp.int32).at[order[jnp.where(places < fixed, places, passed)]].set(jnp.asarray(sizes, jnp.int32))

    sizes = jnp.where(number % 4 == 0, named(crowded, number // 4), named(common, number - number // 4 - 1))
    mixed = jax.random.permutation(jax.random.fold_in(own, 3), count)
    giver, receiver = mixed[0:count // 2 * 2:2], mixed[1:count // 2 * 2:2]
    slack = jnp.minimum(sizes[giver] - 1, limit - sizes[receiver]) // 2
    slack = jnp.where((giver == order[0]) | (receiver == order[0]) | (sizes[receiver] == 0), 0, jnp.maximum(slack, 0))
    passed = jax.random.randint(jax.random.fold_in(own, 4), (count // 2,), 0, 1 << 20) % (slack + 1)
    sizes = sizes.at[giver].add(-passed).at[receiver].add(passed)
    labels = jnp.searchsorted(jnp.cumsum(sizes), jnp.arange(rows * top), side="right").astype(jnp.int32)
    listing = labels.reshape(top, rows).T
    listing = listing[jax.random.permutation(jax.random.fold_in(own, 1), rows)]
    rotation = jax.random.randint(jax.random.fold_in(own, 2), (rows, 1), 0, top)
    return jnp.take_along_axis(listing, (jnp.arange(top)[None, :] + rotation) % top, axis=1)


def portions_of(number_of, total, bound, lean, full):
    weights = [(1 << 20) // math.isqrt(rank ** lean) + 1 for rank in range(1, number_of + 1)]
    largest = bound if full else min(bound, max(-(-total // number_of), total * weights[0] // sum(weights)))
    least = 1 if total - largest >= number_of - 1 else 0
    holding, rest = [largest] + [least] * (number_of - 1), total - largest - least * (number_of - 1)
    while rest > 0:
        movable = [i for i in range(1, number_of) if holding[i] < largest] or [i for i in range(1, number_of) if holding[i] < bound]
        mass, left = sum([weights[i] for i in movable]), rest
        for i in movable:
            addition = min(bound - holding[i], max(1, left * weights[i] // mass), rest)
            holding[i] = holding[i] + addition
            rest = rest - addition
    return np.array(holding)


def centred(key, extent, deviation, reach, shards=(), held_as=jnp.bfloat16):
    level = block_levels(key, extent, shards, -0.22, 0.18) if shards else 1.0
    entries = jax.random.normal(key, extent, jnp.float32) * deviation * level
    return jnp.minimum(jnp.maximum(entries, -reach), reach).astype(held_as)


def setup_inputs(seed: int = 0) -> dict:
    streams_of = jax.random.split(jax.random.key(seed), 9)
    tokens = centred(streams_of[0], (TOKENS, D), 1.0, 6.0, ((0, 32), (1, 8)))
    routing_keys = jax.random.split(jax.random.fold_in(streams_of[1], 1), TOKENS // TOK_DEV)
    routing_turns = jax.random.permutation(jax.random.fold_in(streams_of[1], 3), TOKENS // TOK_DEV)
    routing = jax.vmap(lambda own, number: deal_out(jax.random.fold_in(streams_of[1], 2), own, number, TOK_DEV, EXPERTS, TOPK, CAP, 2))(routing_keys, routing_turns).reshape((TOKENS, TOPK))
    gate_weights = jnp.clip(0.05 + 0.55 * jax.random.uniform(streams_of[2], (TOKENS, TOPK), jnp.float32) ** block_levels(streams_of[2], (TOKENS, TOPK), ((0, 32),), -0.2, 0.2), 0.05, 0.6)
    owner = jax.random.permutation(streams_of[3], EXPERTS).astype(jnp.int32)
    weights = centred(streams_of[4], (EXPERTS, 2, D, FF), D ** -0.5, 0.09375, ((0, 32), (3, 8)))
    grads = centred(streams_of[5], (EXPERTS, 2, D, FF), 1.0, 6.0, ((0, 32), (3, 8)))
    first = centred(streams_of[6], (EXPERTS, 2, D, FF), 0.3, 4.0, ((0, 32), (3, 8)))
    second = jnp.clip(jnp.exp(math.log(2.0) - 3.6927934 * jax.random.uniform(streams_of[7], (EXPERTS, 2, D, FF), jnp.float32) ** block_levels(streams_of[7], (EXPERTS, 2, D, FF), ((0, 32), (3, 8)), -0.2, 0.2)), 0.049804688, 2.0).astype(jnp.bfloat16)
    return {"tokens": tokens, "routing": routing, "gate_weights": gate_weights, "owner": owner, "weights": weights, "grads": grads, "first": first, "second": second}


beta_first = 0.9
beta_second = 0.95
learning_rate = 0.003
weight_decay = 0.1
epsilon = 1e-08

def adamw_step(weights, grads, first, second):
    gradient = grads.astype(jnp.float32)
    first_new = beta_first * first.astype(jnp.float32) + (1.0 - beta_first) * gradient
    second_new = beta_second * second.astype(jnp.float32) + (1.0 - beta_second) * gradient * gradient
    current = weights.astype(jnp.float32)
    updated = current - learning_rate * (first_new / (jnp.sqrt(second_new) + epsilon) + weight_decay * current)
    return (updated.astype(jnp.bfloat16), first_new.astype(jnp.bfloat16), second_new.astype(jnp.bfloat16))

def reference(tokens, routing, gate_weights, owner, weights, grads, first, second):
    updated, first_new, second_new = adamw_step(weights, grads, first, second)
    new_weights = jnp.zeros_like(updated).at[owner].set(updated)
    new_first = jnp.zeros_like(first_new).at[owner].set(first_new)
    new_second = jnp.zeros_like(second_new).at[owner].set(second_new)
    per_block = TOK_DEV * TOPK
    chosen = routing.reshape(N_EXPERT, per_block)
    onehot = (chosen[:, :, None] == jnp.arange(EXPERTS, dtype=jnp.int32)[None, None, :]).astype(jnp.int32)
    earlier = jnp.cumsum(onehot, axis=1) - onehot
    slot_index = lax.optimization_barrier(jnp.sum(earlier * onehot, axis=2)).astype(jnp.int32)
    block_index = jnp.arange(N_EXPERT, dtype=jnp.int32)[:, None]
    column = (block_index * CAP + slot_index).astype(jnp.int32)
    token_index = (block_index * TOK_DEV + jnp.arange(per_block, dtype=jnp.int32)[None, :] // TOPK).astype(jnp.int32)
    table = jnp.full((EXPERTS, N_EXPERT * CAP), TOKENS, jnp.int32).at[chosen, column].set(token_index)
    padded = jnp.concatenate([tokens, jnp.zeros((1, D), tokens.dtype)], axis=0)

    def serve_expert(inputs):
        index_row, expert_state = inputs
        rows_in = jnp.take(padded, index_row, axis=0)
        hidden = jax.nn.silu(jnp.dot(rows_in, expert_state[0], preferred_element_type=jnp.float32)).astype(jnp.bfloat16)
        total = jnp.zeros((rows_in.shape[0], D), jnp.float32)
        for group in range(N_CUTS):
            lower = group * FF_GROUP
            piece = jnp.dot(hidden[:, lower:lower + FF_GROUP], expert_state[1][:, lower:lower + FF_GROUP].T, preferred_element_type=jnp.float32)
            piece = lax.optimization_barrier(piece.astype(jnp.bfloat16))
            total = total + piece.astype(jnp.float32)
        return total.astype(jnp.bfloat16)
    outputs = lax.map(serve_expert, (table, updated))
    flat_index = (chosen * (N_EXPERT * CAP) + column).astype(jnp.int32)
    picked = jnp.take(outputs.reshape(-1, D), flat_index.reshape(-1), axis=0).reshape(TOKENS, TOPK, D)
    mixed = jnp.einsum('tk,tkd->td', gate_weights.astype(jnp.float32), picked.astype(jnp.float32), precision=lax.Precision.HIGHEST)
    return (mixed.astype(jnp.bfloat16), new_weights, new_first, new_second)
```

```python
import jax
import jax.numpy as jnp
from jax import lax
from jax.experimental import pallas as pl
from jax.experimental.pallas import tpu as pltpu
from jax.sharding import PartitionSpec as P

beta_first = 0.9
beta_second = 0.95
learning_rate = 0.003
weight_decay = 0.1
epsilon = 1e-08


def adamw_kernel(weights, grads, first, second, updated_out, first_out, second_out):
    gradient = grads[...].astype(jnp.float32)
    first_new = beta_first * first[...].astype(jnp.float32) + (1.0 - beta_first) * gradient
    second_new = (
        beta_second * second[...].astype(jnp.float32)
        + (1.0 - beta_second) * gradient * gradient
    )
    current = weights[...].astype(jnp.float32)
    updated = current - learning_rate * (
        first_new / (jnp.sqrt(second_new) + epsilon) + weight_decay * current
    )
    updated_out[...] = updated.astype(jnp.bfloat16)
    first_out[...] = first_new.astype(jnp.bfloat16)
    second_out[...] = second_new.astype(jnp.bfloat16)


def adamw(weights, grads, first, second, steps):
    rows, lanes = weights.shape
    block = pl.BlockSpec((rows // steps, lanes), lambda i: (i, 0))
    shape = jax.ShapeDtypeStruct((rows, lanes), jnp.bfloat16)
    return pl.pallas_call(
        adamw_kernel,
        grid=(steps,),
        in_specs=[block] * 4,
        out_specs=[block] * 3,
        out_shape=[shape] * 3,
        cost_estimate=pl.CostEstimate(
            flops=12 * rows * lanes, bytes_accessed=14 * rows * lanes, transcendentals=rows * lanes
        ),
        name="adamw",
    )(weights, grads, first, second)


def up_kernel(rows, weights, out):
    for group in range(weights.shape[0]):
        out[group] = jnp.dot(
            rows[...], weights[group], preferred_element_type=jnp.float32
        ).astype(jnp.bfloat16)


def up_project(rows, weights, steps):
    count, features = rows.shape
    groups, _, width = weights.shape
    return pl.pallas_call(
        up_kernel,
        grid=(steps,),
        in_specs=[
            pl.BlockSpec((count // steps, features), lambda i: (i, 0)),
            pl.BlockSpec((groups, features, width), lambda i: (0, 0, 0)),
        ],
        out_specs=pl.BlockSpec((groups, count // steps, width), lambda i: (0, i, 0)),
        out_shape=jax.ShapeDtypeStruct((groups, count, width), jnp.bfloat16),
        cost_estimate=pl.CostEstimate(
            flops=2 * count * features * groups * width,
            bytes_accessed=2 * (count * features + groups * width * (features + count)),
            transcendentals=0,
        ),
        name="up_project",
    )(rows, weights)


def down_kernel(hidden, weights, out):
    total = jnp.zeros(out.shape, jnp.float32)
    for group in range(weights.shape[0]):
        total += lax.dot_general(
            hidden[group],
            weights[group],
            (((1,), (1,)), ((), ())),
            preferred_element_type=jnp.float32,
        ).astype(jnp.bfloat16).astype(jnp.float32)
    out[...] = total.astype(jnp.bfloat16)


def down_project(hidden, weights, steps):
    groups, count, width = hidden.shape
    features = weights.shape[1]
    return pl.pallas_call(
        down_kernel,
        grid=(steps,),
        in_specs=[
            pl.BlockSpec((groups, count // steps, width), lambda i: (0, i, 0)),
            pl.BlockSpec((groups, features, width), lambda i: (0, 0, 0)),
        ],
        out_specs=pl.BlockSpec((count // steps, features), lambda i: (i, 0)),
        out_shape=jax.ShapeDtypeStruct((count, features), jnp.bfloat16),
        cost_estimate=pl.CostEstimate(
            flops=2 * count * features * groups * width,
            bytes_accessed=2 * (count * features + groups * width * (features + count)),
            transcendentals=0,
        ),
        name="down_project",
    )(hidden, weights)


def exchange(array, axis):
    return lax.all_to_all(array, axis, split_axis=0, concat_axis=0, tiled=True)


def local(tokens, routing, gate_weights, owner, weights, grads, first, second):
    expert_count = owner.shape[0]
    cut_count = lax.axis_size("cuts")
    token_count, features = tokens.shape
    top_count = routing.shape[1]
    capacity = 5 * token_count * top_count // (4 * expert_count)
    state_shape = weights.shape
    width = state_shape[3]
    model = state_shape[2]
    order = jnp.arange(expert_count, dtype=jnp.int32)

    flat = [array.reshape(-1, width) for array in (weights, grads, first, second)]
    updated, first_new, second_new = adamw(*flat, 7)

    matches = routing[:, :, None] == order[None, None, :]
    named = jnp.any(matches, axis=1)
    gate = jnp.sum(jnp.where(matches, gate_weights[:, :, None], 0.0), axis=1)
    positions = jnp.arange(token_count, dtype=jnp.int32)
    earlier = (positions[None, :] < positions[:, None]).astype(jnp.bfloat16)
    slot = jnp.dot(
        earlier, named.astype(jnp.bfloat16), preferred_element_type=jnp.float32
    ).astype(jnp.int32)
    slot = jnp.where(named, slot, -1)
    slots = jnp.arange(capacity, dtype=jnp.int32)
    place = slot.T[:, None, :] == slots[None, :, None]
    buffered = jnp.dot(
        place.astype(jnp.bfloat16).reshape(expert_count * capacity, token_count),
        tokens,
        preferred_element_type=jnp.float32,
    ).astype(jnp.bfloat16)
    incoming = exchange(buffered.reshape(expert_count, capacity, features), "expert")

    split = updated.reshape(2, cut_count, features, width)
    up_block = exchange(split[0], "cuts")
    down_block = exchange(split[1], "cuts")
    parts = up_project(incoming.reshape(-1, features), up_block, 5)
    pre_active = lax.psum_scatter(parts, "cuts", scatter_dimension=0, tiled=False)
    hidden = jax.nn.silu(pre_active.astype(jnp.float32)).astype(jnp.bfloat16)
    every = lax.all_gather(hidden, "cuts", axis=0, tiled=False)
    expert_out = down_project(every, down_block, 5)
    returned = exchange(expert_out.reshape(expert_count, capacity, features), "expert")

    share = jnp.where(
        slot[:, :, None] == slots[None, None, :], gate[:, :, None], 0.0
    ).reshape(token_count, expert_count * capacity)
    mixed = jnp.dot(
        share,
        returned.reshape(expert_count * capacity, features).astype(jnp.float32),
        precision=lax.Precision.HIGHEST,
        preferred_element_type=jnp.float32,
    ).astype(jnp.bfloat16)

    holder = jnp.sum(order[None, :] * (owner[None, :] == order[:, None]), axis=1)
    moved = []
    for array in (updated, first_new, second_new):
        spread = exchange(array.reshape(expert_count, -1, width), "expert")
        arrived = exchange(jnp.take(spread, holder, axis=0), "expert")
        moved.append(arrived.reshape(state_shape))
    return (mixed, *moved)


def solution(mesh):
    state = P("expert", None, None, "cuts")
    return jax.shard_map(
        local,
        mesh=mesh,
        in_specs=(
            P("expert", "cuts"),
            P("expert", None),
            P("expert", None),
            P(),
            state,
            state,
            state,
            state,
        ),
        out_specs=(P("expert", "cuts"), state, state, state),
        check_vma=False,
    )
```

```python
import jax
import jax.numpy as jnp
from jax import lax
from jax.experimental import pallas as pl
from jax.experimental.pallas import tpu as pltpu
from jax.sharding import PartitionSpec as P

beta_first = 0.9
beta_second = 0.95
learning_rate = 0.003
weight_decay = 0.1
epsilon = 1e-08

Y, Z, CORE = 4, 4, 2
PAIR, X = 2, 4


def adamw_kernel(weights, grads, first, second, updated_out, spread_out):
    gradient = grads[...].astype(jnp.float32)
    first_new = beta_first * first[...].astype(jnp.float32) + (1.0 - beta_first) * gradient
    second_new = (
        beta_second * second[...].astype(jnp.float32)
        + (1.0 - beta_second) * gradient * gradient
    )
    current = weights[...].astype(jnp.float32)
    updated = current - learning_rate * (
        first_new / (jnp.sqrt(second_new) + epsilon) + weight_decay * current
    )
    chunks, _, rows, lanes = spread_out.shape
    updated_out[...] = updated.astype(jnp.bfloat16)
    for place, array in enumerate((updated, first_new, second_new)):
        spread_out[:, place] = array.astype(jnp.bfloat16).reshape(chunks, rows, lanes)


def adamw(weights, grads, first, second, chunks, steps):
    rows, lanes = weights.shape
    block = pl.BlockSpec((rows // steps, lanes), lambda i: (i, 0))
    size = rows // chunks
    return pl.pallas_call(
        adamw_kernel,
        grid=(steps,),
        in_specs=[block] * 4,
        out_specs=[
            block,
            pl.BlockSpec((chunks // steps, 3, size, lanes), lambda i: (i, 0, 0, 0)),
        ],
        out_shape=[
            jax.ShapeDtypeStruct((rows, lanes), jnp.bfloat16),
            jax.ShapeDtypeStruct((chunks, 3, size, lanes), jnp.bfloat16),
        ],
        cost_estimate=pl.CostEstimate(
            flops=12 * rows * lanes, bytes_accessed=16 * rows * lanes, transcendentals=rows * lanes
        ),
        name="adamw",
    )(weights, grads, first, second)


def up_kernel(rows, *refs):
    out = refs[-1]
    for place, weight in enumerate(refs[:-1]):
        out[place] = jnp.dot(
            rows[...], weight[...], preferred_element_type=jnp.float32
        ).astype(jnp.bfloat16)


def up_project(rows, blocks, steps):
    count, features = rows.shape
    width = blocks[0].shape[2]
    groups = len(blocks)
    return pl.pallas_call(
        up_kernel,
        grid=(steps,),
        in_specs=[pl.BlockSpec((count // steps, features), lambda i: (i, 0))]
        + [pl.BlockSpec((None, features, width), lambda i: (0, 0, 0))] * groups,
        out_specs=pl.BlockSpec((groups, count // steps, width), lambda i: (0, i, 0)),
        out_shape=jax.ShapeDtypeStruct((groups, count, width), jnp.bfloat16),
        cost_estimate=pl.CostEstimate(
            flops=2 * count * features * groups * width,
            bytes_accessed=2 * (count * features + groups * width * (features + count)),
            transcendentals=0,
        ),
        name="up_project",
    )(rows, *blocks)


def down_kernel(*refs):
    out = refs[-1]
    half = len(refs) // 2
    total = jnp.zeros(out.shape, jnp.float32)
    for hidden, weight in zip(refs[:half], refs[half:-1]):
        total += lax.dot_general(
            hidden[...],
            weight[...],
            (((1,), (1,)), ((), ())),
            preferred_element_type=jnp.float32,
        ).astype(jnp.bfloat16).astype(jnp.float32)
    out[...] = total.astype(jnp.bfloat16)


def down_project(hidden, blocks, steps):
    count, width = hidden[0].shape
    features = blocks[0].shape[1]
    groups = len(blocks)
    return pl.pallas_call(
        down_kernel,
        grid=(steps,),
        in_specs=[pl.BlockSpec((count // steps, width), lambda i: (i, 0))] * groups
        + [pl.BlockSpec((None, features, width), lambda i: (1, 0, 0))] * groups,
        out_specs=pl.BlockSpec((count // steps, features), lambda i: (i, 0)),
        out_shape=jax.ShapeDtypeStruct((count, features), jnp.bfloat16),
        cost_estimate=pl.CostEstimate(
            flops=2 * count * features * groups * width,
            bytes_accessed=2 * (count * features + groups * width * (features + count)),
            transcendentals=0,
        ),
        name="down_project",
    )(*hidden, *blocks)


def order_kernel(array, *refs):
    pass


def after(array, *earlier):
    anywhere = pl.BlockSpec(memory_space=pl.ANY)
    return pl.pallas_call(
        order_kernel,
        in_specs=[anywhere] * (1 + len(earlier)),
        out_specs=anywhere,
        out_shape=jax.ShapeDtypeStruct(array.shape, array.dtype),
        input_output_aliases={0: 0},
        cost_estimate=pl.CostEstimate(flops=0, bytes_accessed=0, transcendentals=0),
        name="after",
    )(array, *earlier)


def expert_index(y, z, core):
    return (y % Y) * (Z * CORE) + (z % Z) * CORE + core


def shift(array, dy=0, dz=0, dcore=0, dpair=0, dx=0):
    if not (dy % Y or dz % Z or dcore or dpair or dx % X):
        return array
    sites = [
        (y, z, core, pair, x)
        for y in range(Y)
        for z in range(Z)
        for core in range(CORE)
        for pair in range(PAIR)
        for x in range(X)
    ]

    def index(y, z, core, pair, x):
        return expert_index(y, z, core) * (PAIR * X) + pair * X + x % X

    pairs = [
        (index(*site), index(site[0] + dy, site[1] + dz, site[2] ^ dcore, site[3] ^ dpair, site[4] + dx))
        for site in sites
    ]
    return lax.ppermute(array, ("expert", "cuts"), pairs)


def exchange(array, axis):
    return lax.all_to_all(array, axis, split_axis=0, concat_axis=0, tiled=True)


def local(tokens, routing, gate_weights, owner, weights, grads, first, second):
    expert_count = owner.shape[0]
    cut_count = lax.axis_size("cuts")
    token_count, features = tokens.shape
    top_count = routing.shape[1]
    capacity = 5 * token_count * top_count // (4 * expert_count)
    state_shape = weights.shape
    width = state_shape[3]
    order = jnp.arange(expert_count, dtype=jnp.int32)
    me = lax.axis_index("expert")
    my_y, my_z, my_core = me // (Z * CORE), (me // CORE) % Z, me % CORE
    cut = lax.axis_index("cuts")
    my_pair, my_x = cut // X, cut % X
    plane = [(dcore, dy) for dcore in range(CORE) for dy in range(Y)]
    flat = [array.reshape(-1, width) for array in (weights, grads, first, second)]
    updated, spread = adamw(*flat, expert_count, 16)

    turned = routing.T[None]
    gates_of = gate_weights.T[None]
    near_parts, far_parts, gate_parts = [], [], []
    for dz in range(Z):
        ids = jnp.stack(
            [
                expert_index(my_y + dy, my_z + dz, my_core ^ dcore)
                for dcore, dy in plane
            ]
        ).astype(jnp.int32)
        matches = turned == ids[:, None, None]
        gate = jnp.sum(jnp.where(matches, gates_of, 0.0), axis=1)
        gate = jnp.where(jnp.any(matches, axis=1), gate, -1.0)
        gate_parts.append(shift(gate, dz=dz))
        near_parts.append(shift(tokens, dz=dz))
        far_parts.append(shift(tokens, dz=dz, dpair=1))

    positions = jnp.arange(token_count, dtype=jnp.int32)
    earlier = (positions[:, None] < positions[None, :]).astype(jnp.bfloat16)
    all_gates = jnp.stack(gate_parts, axis=1)
    named = all_gates >= 0.0
    slot = jnp.einsum(
        "ezu,ut->ezt", named.astype(jnp.bfloat16), earlier, preferred_element_type=jnp.float32
    ).astype(jnp.int32)
    slot = slot + capacity * jnp.arange(Z, dtype=jnp.int32)[None, :, None]
    slot = jnp.where(named, slot, -1).reshape(len(plane), Z * token_count)
    slots = jnp.arange(Z * capacity, dtype=jnp.int32)
    place = (slot[:, None, :] == slots[None, :, None]).astype(jnp.bfloat16)
    near = jnp.concatenate(near_parts, axis=0)
    far = jnp.concatenate(far_parts, axis=0)
    chosen = place.reshape(len(plane) * Z * capacity, Z * token_count)
    buffered = jnp.concatenate(
        [
            jnp.dot(chosen, part, preferred_element_type=jnp.float32).astype(jnp.bfloat16)
            for part in (near, far)
        ],
        axis=1,
    ).reshape(len(plane), Z * capacity, 2 * features)
    incoming = [
        shift(buffered[j], dy=dy, dcore=dcore)
        for j, (dcore, dy) in enumerate(plane)
    ]

    spread = exchange(after(spread, *gate_parts, *near_parts, *far_parts), "expert")

    by_cut = updated.reshape(2, cut_count, features, width)
    blocks = []
    for dx in range(X):
        block = jnp.concatenate(
            [
                lax.dynamic_slice_in_dim(by_cut, pair * X + (my_x + dx) % X, 1, axis=1)[:, 0]
                for pair in (my_pair, my_pair ^ 1)
            ],
            axis=1,
        )
        blocks.append(shift(block, dx=dx))

    parts = up_project(jnp.concatenate(incoming, axis=0), blocks, 5)
    sums = [shift(parts[dx], dx=-dx) for dx in range(X)]
    total = sum(part.astype(jnp.float32) for part in sums)
    hidden = jax.nn.silu(total).astype(jnp.bfloat16)

    holder = jnp.sum(order[None, :] * (owner[None, :] == order[:, None]), axis=1)
    outgoing = jnp.take(spread, holder, axis=0, mode="clip")
    arrived = exchange(after(outgoing, hidden), "expert")

    every = [shift(hidden, dx=dx) for dx in range(X)]
    expert_out = down_project(every, blocks, 5).reshape(len(plane), Z * capacity, 2 * features)
    returned = jnp.concatenate(
        [
            shift(expert_out[j], dy=-dy, dcore=dcore)
            for j, (dcore, dy) in enumerate(plane)
        ],
        axis=0,
    )

    spots = slot[:, :, None] == slots[None, None, :]
    gate = all_gates.reshape(len(plane), Z * token_count)
    high = gate.astype(jnp.bfloat16)
    low = (gate - high.astype(jnp.float32)).astype(jnp.bfloat16)
    shares = [
        jnp.where(spots, half[:, :, None], jnp.zeros((), jnp.bfloat16))
        .transpose(1, 0, 2)
        .reshape(Z * token_count, -1)
        for half in (high, low)
    ]
    partial = sum(jnp.dot(share, returned, preferred_element_type=jnp.float32) for share in shares)
    partial = partial.astype(jnp.bfloat16).reshape(Z, token_count, PAIR, features)
    mixed = sum(
        shift(partial[dz, :, dpair], dz=-dz, dpair=dpair).astype(jnp.float32)
        for dz in range(Z)
        for dpair in range(PAIR)
    ).astype(jnp.bfloat16)
    moved = [arrived[:, place].reshape(state_shape) for place in range(3)]
    return (mixed, *moved)


def solution(mesh):
    state = P("expert", None, None, "cuts")
    return jax.shard_map(
        local,
        mesh=mesh,
        in_specs=(
            P("expert", "cuts"),
            P("expert", None),
            P("expert", None),
            P(),
            state,
            state,
            state,
            state,
        ),
        out_specs=(P("expert", "cuts"), state, state, state),
        check_vma=False,
    )
```

```python
import functools

import jax
import jax.numpy as jnp
from jax import lax
from jax.experimental import pallas as pl
from jax.experimental.pallas import tpu as pltpu
from jax.sharding import PartitionSpec as P

beta_first = 0.9
beta_second = 0.95
learning_rate = 0.003
weight_decay = 0.1
epsilon = 1e-08

Y, Z, CORE = 4, 4, 2
PAIR, X = 2, 4


def expert_index(y, z, core):
    return (y % Y) * (Z * CORE) + (z % Z) * CORE + core


def shift(array, dy=0, dz=0, dcore=0, dpair=0, dx=0):
    if not (dy % Y or dz % Z or dcore or dpair or dx % X):
        return array
    sites = [
        (y, z, core, pair, x)
        for y in range(Y)
        for z in range(Z)
        for core in range(CORE)
        for pair in range(PAIR)
        for x in range(X)
    ]

    def index(y, z, core, pair, x):
        return expert_index(y, z, core) * (PAIR * X) + pair * X + x % X

    pairs = [
        (index(*site), index(site[0] + dy, site[1] + dz, site[2] ^ dcore, site[3] ^ dpair, site[4] + dx))
        for site in sites
    ]
    return lax.ppermute(array, ("expert", "cuts"), pairs)


def adamw_kernel(weights, grads, first, second, out):
    gradient = grads[...].astype(jnp.float32)
    first_new = beta_first * first[...].astype(jnp.float32) + (1.0 - beta_first) * gradient
    second_new = (
        beta_second * second[...].astype(jnp.float32)
        + (1.0 - beta_second) * gradient * gradient
    )
    current = weights[...].astype(jnp.float32)
    root = second_new * lax.rsqrt(second_new)
    updated = current - learning_rate * (first_new / (root + epsilon) + weight_decay * current)
    for place, array in enumerate((updated, first_new, second_new)):
        out[:, place] = array.astype(jnp.bfloat16)


def adamw(weights, grads, first, second, steps):
    chunks, rows, lanes = weights.shape
    block = pl.BlockSpec((chunks // steps, rows, lanes), lambda i: (i, 0, 0))
    elements = chunks * rows * lanes
    return pl.pallas_call(
        adamw_kernel,
        grid=(steps,),
        in_specs=[block] * 4,
        out_specs=pl.BlockSpec((chunks // steps, 3, rows, lanes), lambda i: (i, 0, 0, 0)),
        out_shape=jax.ShapeDtypeStruct((chunks, 3, rows, lanes), jnp.bfloat16),
        cost_estimate=pl.CostEstimate(
            flops=12 * elements, bytes_accessed=14 * elements, transcendentals=elements
        ),
        name="adamw",
    )(weights, grads, first, second)


def order_kernel(array, *refs):
    pass


def after(array, *earlier):
    anywhere = pl.BlockSpec(memory_space=pl.ANY)
    return pl.pallas_call(
        order_kernel,
        in_specs=[anywhere] * (1 + len(earlier)),
        out_specs=anywhere,
        out_shape=jax.ShapeDtypeStruct(array.shape, array.dtype),
        input_output_aliases={0: 0},
        cost_estimate=pl.CostEstimate(flops=0, bytes_accessed=0, transcendentals=0),
        name="after",
    )(array, *earlier)


def exchange(array):
    return lax.all_to_all(array, "expert", split_axis=0, concat_axis=0, tiled=True)


def whole(kernel, inputs, shapes, flops, name, scratch=()):
    sizes = [array.size * array.dtype.itemsize for array in (*inputs, *shapes)]
    vmem = pl.BlockSpec(memory_space=pltpu.VMEM)
    return pl.pallas_call(
        kernel,
        in_specs=[vmem] * len(inputs),
        out_specs=[vmem] * len(shapes),
        out_shape=shapes,
        scratch_shapes=scratch,
        compiler_params=pltpu.CompilerParams(vmem_limit_bytes=40 * 2**20),
        cost_estimate=pl.CostEstimate(flops=flops, bytes_accessed=sum(sizes), transcendentals=0),
        name=name,
    )(*inputs)


def dispatch_kernel(slot, tokens, *outs):
    for place in range(slot.shape[0]):
        out = outs[place % Y].at[place // Y]
        rows = lax.broadcasted_iota(jnp.int32, (out.shape[0], slot.shape[1]), 0)
        chosen = jnp.where(slot[place : place + 1, :] == rows, 1.0, 0.0).astype(jnp.bfloat16)
        out[...] = jnp.dot(chosen, tokens[...], preferred_element_type=jnp.float32).astype(
            jnp.bfloat16
        )


def dispatch(slot, tokens, rows):
    shape = jax.ShapeDtypeStruct((CORE, rows, tokens.shape[1]), jnp.bfloat16)
    flops = 200 * slot.shape[0] * rows * tokens.size
    return whole(dispatch_kernel, [slot, tokens], [shape] * Y, flops, "dispatch")


def plane_shift(parts, sign, earlier=()):
    arrived = [shift(part, dy=sign * dy) for dy, part in enumerate(parts)]
    swapped = jnp.stack([part[1] for part in arrived])
    if earlier:
        swapped = after(swapped, *earlier)
    return [*arrived, shift(swapped, dcore=1)]


def rows_of(refs):
    return [ref.at[0] for ref in refs[:Y]] + [refs[Y].at[dy] for dy in range(Y)]


def up_kernel(*refs):
    rows, blocks = rows_of(refs), refs[Y + 1 : Y + 1 + X]
    outs, joined = refs[Y + 1 + X : -1], refs[-1]
    width = outs[0].shape[1]
    for number, block in enumerate(blocks):
        joined[:, number * width : (number + 1) * width] = block[...]
    for place, part in enumerate(rows):
        count = part.shape[0]
        product = jnp.dot(part[...], joined[...], preferred_element_type=jnp.float32)
        for number, out in enumerate(outs):
            out[place * count : (place + 1) * count, :] = product[
                :, number * width : (number + 1) * width
            ].astype(jnp.bfloat16)


def up_project(rows, blocks):
    features, width = blocks[0].shape
    count = Y * CORE * rows[0].shape[1]
    return whole(
        up_kernel,
        [*rows, *blocks],
        [jax.ShapeDtypeStruct((count, width), jnp.bfloat16)] * len(blocks),
        2 * count * features * width * len(blocks),
        "up_project",
        [pltpu.VMEM((features, len(blocks) * width), jnp.bfloat16)],
    )


def down_kernel(*refs):
    hidden, blocks, outs, joined = refs[:X], refs[X : 2 * X], refs[2 * X : -1], refs[-1]
    width = hidden[0].shape[1]
    for number, block in enumerate(blocks):
        joined[:, number * width : (number + 1) * width] = block[...]
    for place in range(Y * CORE):
        out = outs[place % Y].at[place // Y]
        count = out.shape[0]
        rows = jnp.concatenate(
            [part[place * count : (place + 1) * count, :] for part in hidden], axis=1
        )
        out[...] = lax.dot_general(
            rows, joined[...], (((1,), (1,)), ((), ())), preferred_element_type=jnp.float32
        ).astype(jnp.bfloat16)


def down_project(hidden, blocks):
    features, width = blocks[0].shape
    count = hidden[0].shape[0]
    return whole(
        down_kernel,
        [*hidden, *blocks],
        [jax.ShapeDtypeStruct((CORE, count // (Y * CORE), features), jnp.bfloat16)] * Y,
        2 * count * features * width * len(blocks),
        "down_project",
        [pltpu.VMEM((features, len(blocks) * width), jnp.bfloat16)],
    )


def combine_kernel(slot, high, low, *refs):
    outputs, out = rows_of(refs), refs[-1]
    total = jnp.zeros(out.shape, jnp.float32)
    for place, part in enumerate(outputs):
        rows = lax.broadcasted_iota(jnp.int32, (part.shape[0], slot.shape[1]), 0)
        found = slot[place : place + 1, :] == rows
        for gate in (high, low):
            share = jnp.where(found, gate[place : place + 1, :], 0.0).astype(jnp.bfloat16)
            total += lax.dot_general(
                share, part[...], (((0,), (0,)), ((), ())), preferred_element_type=jnp.float32
            )
    out[...] = total


def combine(slot, high, low, outputs):
    tokens, features = slot.shape[1], outputs[0].shape[2]
    flops = 4 * slot.size * outputs[0].shape[1] * features
    shape = jax.ShapeDtypeStruct((tokens, features), jnp.float32)
    return whole(combine_kernel, [slot, high, low, *outputs], [shape], flops, "combine")[0]


def local(tokens, routing, gate_weights, owner, weights, grads, first, second):
    expert_count = owner.shape[0]
    cut_count = lax.axis_size("cuts")
    token_count, features = tokens.shape
    top_count = routing.shape[1]
    capacity = 5 * token_count * top_count // (4 * expert_count)
    state_shape = weights.shape
    width = state_shape[3]
    me = lax.axis_index("expert")
    my_y, my_z, my_core = me // (Z * CORE), (me // CORE) % Z, me % CORE
    cut = lax.axis_index("cuts")
    my_pair, my_x = cut // X, cut % X
    plane = [(dcore, dy) for dcore in range(CORE) for dy in range(Y)]
    pieces = [
        array.reshape(expert_count, -1, width) for array in (weights, grads, first, second)
    ]
    state = adamw(*pieces, 8)
    order = jnp.arange(expert_count, dtype=jnp.int32)
    matches = routing[:, None, :] == order[None, :, None]
    gate = jnp.sum(jnp.where(matches, gate_weights[:, None, :], 0.0), axis=2)
    gate = jnp.where(jnp.any(matches, axis=2), gate, -1.0)
    high = gate.astype(jnp.bfloat16)
    low = (gate - high.astype(jnp.float32)).astype(jnp.bfloat16)
    wide = jnp.concatenate([tokens, shift(tokens, dpair=1), high, low], axis=1)
    near = [shift(wide, dz=dz) for dz in range(Z)]
    spread = exchange(state)
    near = jnp.concatenate(near, axis=0)
    gates = near[:, 2 * features :].T.astype(jnp.float32)
    gates = gates.reshape(2, Y, Z, CORE, Z * token_count)
    gates = lax.dynamic_index_in_dim(gates, my_z, axis=2, keepdims=False)
    high, low = (
        jnp.stack(
            [
                lax.dynamic_slice(
                    part, ((my_y + dy) % Y, my_core ^ dcore, 0), (1, 1, Z * token_count)
                )[0, 0]
                for dcore, dy in plane
            ]
        )
        for part in gates
    )
    near = near[:, : 2 * features]

    positions = jnp.arange(token_count, dtype=jnp.int32)
    earlier = (positions[:, None] < positions[None, :]).astype(jnp.bfloat16)
    named = (high >= 0.0).reshape(len(plane) * Z, token_count)
    slot = jnp.dot(
        named.astype(jnp.bfloat16), earlier, preferred_element_type=jnp.float32
    ).astype(jnp.int32)
    slot = slot + capacity * (jnp.arange(len(plane) * Z, dtype=jnp.int32) % Z)[:, None]
    slot = jnp.where(named, slot, -1).reshape(len(plane), Z * token_count)
    buffered = dispatch(slot, near, Z * capacity)

    by_cut = state[:, 0].reshape(2, cut_count, features, width)
    blocks = []
    for dx in range(X):
        block = jnp.concatenate(
            [
                lax.dynamic_slice_in_dim(by_cut, pair * X + (my_x + dx) % X, 1, axis=1)[:, 0]
                for pair in (my_pair, my_pair ^ 1)
            ],
            axis=1,
        )
        blocks.append(shift(block, dx=dx))

    incoming = plane_shift(buffered, 1, blocks)

    parts = up_project(incoming, [block[0] for block in blocks])
    total = sum(shift(part, dx=-dx).astype(jnp.float32) for dx, part in enumerate(parts))
    hidden = jax.nn.silu(total).astype(jnp.bfloat16)

    every = [shift(hidden, dx=dx) for dx in range(X)]
    expert_out = down_project(every, [block[1] for block in blocks])

    holder = jnp.sum(order[None, :] * (owner[None, :] == order[:, None]), axis=1)
    arrived = exchange(after(jnp.take(spread, holder, axis=0, mode="clip"), expert_out[0]))

    returned = plane_shift(expert_out, -1)

    partial = combine(slot, high, low, returned)
    partial = partial.astype(jnp.bfloat16).reshape(Z, token_count, PAIR, features)
    moved = [arrived[:, place].reshape(state_shape) for place in range(3)]
    mixed = sum(
        shift(partial[dz, :, dpair], dz=-dz, dpair=dpair).astype(jnp.float32)
        for dz in range(Z)
        for dpair in range(PAIR)
        if dz or dpair
    )
    mixed += after(partial[0, :, 0], *moved).astype(jnp.float32)
    return (mixed.astype(jnp.bfloat16), *moved)


def solution(mesh):
    state = P("expert", None, None, "cuts")
    return jax.shard_map(
        local,
        mesh=mesh,
        in_specs=(
            P("expert", "cuts"),
            P("expert", None),
            P("expert", None),
            P(),
            state,
            state,
            state,
            state,
        ),
        out_specs=(P("expert", "cuts"), state, state, state),
        check_vma=False,
    )
```

```python
import functools

import jax
import jax.numpy as jnp
from jax import lax
from jax.experimental import pallas as pl
from jax.experimental.pallas import tpu as pltpu
from jax.sharding import PartitionSpec as P

beta_first = 0.9
beta_second = 0.95
learning_rate = 0.003
weight_decay = 0.1
epsilon = 1e-08

Y, Z, CORE = 4, 4, 2
PAIR, X = 2, 4


def expert_index(y, z, core):
    return (y % Y) * (Z * CORE) + (z % Z) * CORE + core


def shift(array, dy=0, dz=0, dcore=0, dpair=0, dx=0):
    if not (dy % Y or dz % Z or dcore or dpair or dx % X):
        return array
    sites = [
        (y, z, core, pair, x)
        for y in range(Y)
        for z in range(Z)
        for core in range(CORE)
        for pair in range(PAIR)
        for x in range(X)
    ]

    def index(y, z, core, pair, x):
        return expert_index(y, z, core) * (PAIR * X) + pair * X + x % X

    pairs = [
        (index(*site), index(site[0] + dy, site[1] + dz, site[2] ^ dcore, site[3] ^ dpair, site[4] + dx))
        for site in sites
    ]
    return lax.ppermute(array, ("expert", "cuts"), pairs)


def adamw_kernel(weights, grads, first, second, out):
    gradient = grads[...].astype(jnp.float32)
    first_new = beta_first * first[...].astype(jnp.float32) + (1.0 - beta_first) * gradient
    second_new = (
        beta_second * second[...].astype(jnp.float32)
        + (1.0 - beta_second) * gradient * gradient
    )
    current = weights[...].astype(jnp.float32)
    root = second_new * lax.rsqrt(second_new)
    updated = current - learning_rate * (first_new / (root + epsilon) + weight_decay * current)
    for place, array in enumerate((updated, first_new, second_new)):
        out[:, place] = array.astype(jnp.bfloat16)


def adamw(weights, grads, first, second, steps):
    chunks, rows, lanes = weights.shape
    block = pl.BlockSpec((chunks // steps, rows, lanes), lambda i: (i, 0, 0))
    elements = chunks * rows * lanes
    return pl.pallas_call(
        adamw_kernel,
        grid=(steps,),
        in_specs=[block] * 4,
        out_specs=pl.BlockSpec((chunks // steps, 3, rows, lanes), lambda i: (i, 0, 0, 0)),
        out_shape=jax.ShapeDtypeStruct((chunks, 3, rows, lanes), jnp.bfloat16),
        cost_estimate=pl.CostEstimate(
            flops=12 * elements, bytes_accessed=14 * elements, transcendentals=elements
        ),
        name="adamw",
    )(weights, grads, first, second)


def order_kernel(array, *refs):
    pass


def after(array, *earlier):
    anywhere = pl.BlockSpec(memory_space=pl.ANY)
    return pl.pallas_call(
        order_kernel,
        in_specs=[anywhere] * (1 + len(earlier)),
        out_specs=anywhere,
        out_shape=jax.ShapeDtypeStruct(array.shape, array.dtype),
        input_output_aliases={0: 0},
        cost_estimate=pl.CostEstimate(flops=0, bytes_accessed=0, transcendentals=0),
        name="after",
    )(array, *earlier)


def exchange(array):
    return lax.all_to_all(array, "expert", split_axis=0, concat_axis=0, tiled=True)


def whole(kernel, inputs, shapes, flops, name, scratch=()):
    sizes = [array.size * array.dtype.itemsize for array in (*inputs, *shapes)]
    vmem = pl.BlockSpec(memory_space=pltpu.VMEM)
    return pl.pallas_call(
        kernel,
        in_specs=[vmem] * len(inputs),
        out_specs=[vmem] * len(shapes),
        out_shape=shapes,
        scratch_shapes=scratch,
        compiler_params=pltpu.CompilerParams(vmem_limit_bytes=40 * 2**20),
        cost_estimate=pl.CostEstimate(flops=flops, bytes_accessed=sum(sizes), transcendentals=0),
        name=name,
    )(*inputs)


def dispatch_kernel(slot, tokens, *outs):
    for place in range(slot.shape[0]):
        out = outs[place % Y].at[place // Y]
        rows = lax.broadcasted_iota(jnp.int32, (out.shape[0], slot.shape[1]), 0)
        chosen = jnp.where(slot[place : place + 1, :] == rows, 1.0, 0.0).astype(jnp.bfloat16)
        out[...] = jnp.dot(chosen, tokens[...], preferred_element_type=jnp.float32).astype(
            jnp.bfloat16
        )


def dispatch(slot, tokens, rows):
    shape = jax.ShapeDtypeStruct((CORE, rows, tokens.shape[1]), jnp.bfloat16)
    flops = 200 * slot.shape[0] * rows * tokens.size
    return whole(dispatch_kernel, [slot, tokens], [shape] * Y, flops, "dispatch")


def plane_shift(parts, sign, earlier=()):
    arrived = [shift(part, dy=sign * dy) for dy, part in enumerate(parts)]
    swapped = jnp.stack([part[1] for part in arrived])
    if earlier:
        swapped = after(swapped, *earlier)
    return [*arrived, shift(swapped, dcore=1)]


def rows_of(refs):
    return [ref.at[0] for ref in refs[:Y]] + [refs[Y].at[dy] for dy in range(Y)]


def up_kernel(*refs):
    rows, blocks = rows_of(refs), refs[Y + 1 : Y + 1 + X]
    outs, joined = refs[Y + 1 + X : -1], refs[-1]
    width = outs[0].shape[1]
    for number, block in enumerate(blocks):
        joined[:, number * width : (number + 1) * width] = block[...]
    for place, part in enumerate(rows):
        count = part.shape[0]
        product = jnp.dot(part[...], joined[...], preferred_element_type=jnp.float32)
        for number, out in enumerate(outs):
            out[place * count : (place + 1) * count, :] = product[
                :, number * width : (number + 1) * width
            ].astype(jnp.bfloat16)


def up_project(rows, blocks):
    features, width = blocks[0].shape
    count = Y * CORE * rows[0].shape[1]
    return whole(
        up_kernel,
        [*rows, *blocks],
        [jax.ShapeDtypeStruct((count, width), jnp.bfloat16)] * len(blocks),
        2 * count * features * width * len(blocks),
        "up_project",
        [pltpu.VMEM((features, len(blocks) * width), jnp.bfloat16)],
    )


def down_kernel(*refs):
    hidden, blocks, outs, joined = refs[:X], refs[X : 2 * X], refs[2 * X : -1], refs[-1]
    width = hidden[0].shape[1]
    for number, block in enumerate(blocks):
        joined[:, number * width : (number + 1) * width] = block[...]
    for place in range(Y * CORE):
        out = outs[place % Y].at[place // Y]
        count = out.shape[0]
        rows = jnp.concatenate(
            [part[place * count : (place + 1) * count, :] for part in hidden], axis=1
        )
        out[...] = lax.dot_general(
            rows, joined[...], (((1,), (1,)), ((), ())), preferred_element_type=jnp.float32
        ).astype(jnp.bfloat16)


def down_project(hidden, blocks):
    features, width = blocks[0].shape
    count = hidden[0].shape[0]
    return whole(
        down_kernel,
        [*hidden, *blocks],
        [jax.ShapeDtypeStruct((CORE, count // (Y * CORE), features), jnp.bfloat16)] * Y,
        2 * count * features * width * len(blocks),
        "down_project",
        [pltpu.VMEM((features, len(blocks) * width), jnp.bfloat16)],
    )


def combine_kernel(slot, high, low, *refs):
    outputs, outs = rows_of(refs), refs[Y + 1 :]
    features, tokens = outs[0].shape
    total = jnp.zeros((PAIR * features, slot.shape[1]), jnp.float32)
    for place, part in enumerate(outputs):
        rows = lax.broadcasted_iota(jnp.int32, (part.shape[0], slot.shape[1]), 0)
        found = slot[place : place + 1, :] == rows
        for gate in (high, low):
            share = jnp.where(found, gate[place : place + 1, :], 0.0).astype(jnp.bfloat16)
            total += lax.dot_general(
                part[...], share, (((0,), (0,)), ((), ())), preferred_element_type=jnp.float32
            )
    for number, out in enumerate(outs):
        source, half = number // PAIR, number % PAIR
        out[...] = total[
            half * features : (half + 1) * features, source * tokens : (source + 1) * tokens
        ].astype(jnp.bfloat16)


def combine(slot, high, low, outputs):
    tokens, features = slot.shape[1], outputs[0].shape[2]
    flops = 4 * slot.size * outputs[0].shape[1] * features
    shape = jax.ShapeDtypeStruct((features // PAIR, tokens // Z), jnp.bfloat16)
    return whole(
        combine_kernel, [slot, high, low, *outputs], [shape] * (Z * PAIR), flops, "combine"
    )


def local(tokens, routing, gate_weights, owner, weights, grads, first, second):
    expert_count = owner.shape[0]
    cut_count = lax.axis_size("cuts")
    token_count, features = tokens.shape
    top_count = routing.shape[1]
    capacity = 5 * token_count * top_count // (4 * expert_count)
    state_shape = weights.shape
    width = state_shape[3]
    me = lax.axis_index("expert")
    my_y, my_z, my_core = me // (Z * CORE), (me // CORE) % Z, me % CORE
    cut = lax.axis_index("cuts")
    my_pair, my_x = cut // X, cut % X
    plane = [(dcore, dy) for dcore in range(CORE) for dy in range(Y)]
    pieces = [
        array.reshape(expert_count, -1, width) for array in (weights, grads, first, second)
    ]
    state = adamw(*pieces, 8)
    order = jnp.arange(expert_count, dtype=jnp.int32)
    matches = routing[:, None, :] == order[None, :, None]
    gate = jnp.sum(jnp.where(matches, gate_weights[:, None, :], 0.0), axis=2)
    gate = jnp.where(jnp.any(matches, axis=2), gate, -1.0)
    high = gate.astype(jnp.bfloat16)
    low = (gate - high.astype(jnp.float32)).astype(jnp.bfloat16)
    wide = jnp.concatenate([tokens, shift(tokens, dpair=1), high, low], axis=1)
    near = [shift(wide, dz=dz) for dz in range(Z)]
    spread = exchange(state)
    near = jnp.concatenate(near, axis=0)
    gates = near[:, 2 * features :].T.astype(jnp.float32)
    gates = gates.reshape(2, Y, Z, CORE, Z * token_count)
    gates = lax.dynamic_index_in_dim(gates, my_z, axis=2, keepdims=False)
    high, low = (
        jnp.stack(
            [
                lax.dynamic_slice(
                    part, ((my_y + dy) % Y, my_core ^ dcore, 0), (1, 1, Z * token_count)
                )[0, 0]
                for dcore, dy in plane
            ]
        )
        for part in gates
    )
    near = near[:, : 2 * features]

    positions = jnp.arange(token_count, dtype=jnp.int32)
    earlier = (positions[:, None] < positions[None, :]).astype(jnp.bfloat16)
    named = (high >= 0.0).reshape(len(plane) * Z, token_count)
    slot = jnp.dot(
        named.astype(jnp.bfloat16), earlier, preferred_element_type=jnp.float32
    ).astype(jnp.int32)
    slot = slot + capacity * (jnp.arange(len(plane) * Z, dtype=jnp.int32) % Z)[:, None]
    slot = jnp.where(named, slot, -1).reshape(len(plane), Z * token_count)
    buffered = dispatch(slot, near, Z * capacity)

    by_cut = state[:, 0].reshape(2, cut_count, features, width)
    blocks = []
    for dx in range(X):
        block = jnp.concatenate(
            [
                lax.dynamic_slice_in_dim(by_cut, pair * X + (my_x + dx) % X, 1, axis=1)[:, 0]
                for pair in (my_pair, my_pair ^ 1)
            ],
            axis=1,
        )
        blocks.append(shift(block, dx=dx))

    incoming = plane_shift(buffered, 1, blocks)

    parts = up_project(incoming, [block[0] for block in blocks])
    total = sum(shift(part, dx=-dx).astype(jnp.float32) for dx, part in enumerate(parts))
    hidden = jax.nn.silu(total).astype(jnp.bfloat16)

    every = [shift(hidden, dx=dx) for dx in range(X)]

    holder = jnp.sum(order[None, :] * (owner[None, :] == order[:, None]), axis=1)
    holder = after(holder, hidden)
    arrived = exchange(jnp.take(spread, holder, axis=0, mode="clip"))

    expert_out = down_project(every, [block[1] for block in blocks])

    returned = plane_shift(expert_out, -1)

    partial = combine(slot, high, low, returned)
    moved = [arrived[:, place].reshape(state_shape) for place in range(3)]
    mixed = sum(
        shift(part, dz=-(number // PAIR), dpair=number % PAIR).astype(jnp.float32)
        for number, part in enumerate(partial)
        if number
    )
    mixed = (mixed + after(partial[0], *moved).astype(jnp.float32)).T
    return (mixed.astype(jnp.bfloat16), *moved)


def solution(mesh):
    state = P("expert", None, None, "cuts")
    return jax.shard_map(
        local,
        mesh=mesh,
        in_specs=(
            P("expert", "cuts"),
            P("expert", None),
            P("expert", None),
            P(),
            state,
            state,
            state,
            state,
        ),
        out_specs=(P("expert", "cuts"), state, state, state),
        check_vma=False,
    )
```

```python
import functools

import jax
import jax.numpy as jnp
from jax import lax
from jax.experimental import pallas as pl
from jax.experimental.pallas import tpu as pltpu
from jax.sharding import PartitionSpec as P

beta_first = 0.9
beta_second = 0.95
learning_rate = 0.003
weight_decay = 0.1
epsilon = 1e-08

Y, Z, CORE = 4, 4, 2
PAIR, X = 2, 4


def expert_index(y, z, core):
    return (y % Y) * (Z * CORE) + (z % Z) * CORE + core


def shift(array, dy=0, dz=0, dcore=0, dpair=0, dx=0):
    if not (dy % Y or dz % Z or dcore or dpair or dx % X):
        return array
    sites = [
        (y, z, core, pair, x)
        for y in range(Y)
        for z in range(Z)
        for core in range(CORE)
        for pair in range(PAIR)
        for x in range(X)
    ]

    def index(y, z, core, pair, x):
        return expert_index(y, z, core) * (PAIR * X) + pair * X + x % X

    pairs = [
        (index(*site), index(site[0] + dy, site[1] + dz, site[2] ^ dcore, site[3] ^ dpair, site[4] + dx))
        for site in sites
    ]
    return lax.ppermute(array, ("expert", "cuts"), pairs)


def adamw_kernel(weights, grads, first, second, out):
    gradient = grads[...].astype(jnp.float32)
    first_new = beta_first * first[...].astype(jnp.float32) + (1.0 - beta_first) * gradient
    second_new = (
        beta_second * second[...].astype(jnp.float32)
        + (1.0 - beta_second) * gradient * gradient
    )
    current = weights[...].astype(jnp.float32)
    root = second_new * lax.rsqrt(second_new)
    updated = current - learning_rate * (first_new / (root + epsilon) + weight_decay * current)
    for place, array in enumerate((updated, first_new, second_new)):
        out[:, place] = array.astype(jnp.bfloat16)


def adamw(weights, grads, first, second, steps):
    chunks, rows, lanes = weights.shape
    block = pl.BlockSpec((chunks // steps, rows, lanes), lambda i: (i, 0, 0))
    elements = chunks * rows * lanes
    return pl.pallas_call(
        adamw_kernel,
        grid=(steps,),
        in_specs=[block] * 4,
        out_specs=pl.BlockSpec((chunks // steps, 3, rows, lanes), lambda i: (i, 0, 0, 0)),
        out_shape=jax.ShapeDtypeStruct((chunks, 3, rows, lanes), jnp.bfloat16),
        cost_estimate=pl.CostEstimate(
            flops=12 * elements, bytes_accessed=14 * elements, transcendentals=elements
        ),
        name="adamw",
    )(weights, grads, first, second)


def order_kernel(array, *refs):
    pass


def after(array, *earlier):
    anywhere = pl.BlockSpec(memory_space=pl.ANY)
    return pl.pallas_call(
        order_kernel,
        in_specs=[anywhere] * (1 + len(earlier)),
        out_specs=anywhere,
        out_shape=jax.ShapeDtypeStruct(array.shape, array.dtype),
        input_output_aliases={0: 0},
        cost_estimate=pl.CostEstimate(flops=0, bytes_accessed=0, transcendentals=0),
        name="after",
    )(array, *earlier)


def exchange(array):
    return lax.all_to_all(array, "expert", split_axis=0, concat_axis=0, tiled=True)


def whole(kernel, inputs, shapes, flops, name, scratch=()):
    sizes = [array.size * array.dtype.itemsize for array in (*inputs, *shapes)]
    vmem = pl.BlockSpec(memory_space=pltpu.VMEM)
    return pl.pallas_call(
        kernel,
        in_specs=[vmem] * len(inputs),
        out_specs=[vmem] * len(shapes),
        out_shape=shapes,
        scratch_shapes=scratch,
        compiler_params=pltpu.CompilerParams(vmem_limit_bytes=40 * 2**20),
        cost_estimate=pl.CostEstimate(flops=flops, bytes_accessed=sum(sizes), transcendentals=0),
        name=name,
    )(*inputs)


def dispatch_kernel(slot, tokens, *outs):
    for place in range(slot.shape[0]):
        out = outs[place % Y].at[place // Y]
        rows = lax.broadcasted_iota(jnp.int32, (out.shape[0], slot.shape[1]), 0)
        chosen = jnp.where(slot[place : place + 1, :] == rows, 1.0, 0.0).astype(jnp.bfloat16)
        out[...] = jnp.dot(chosen, tokens[...], preferred_element_type=jnp.float32).astype(
            jnp.bfloat16
        )


def dispatch(slot, tokens, rows):
    shape = jax.ShapeDtypeStruct((CORE, rows, tokens.shape[1]), jnp.bfloat16)
    flops = 200 * slot.shape[0] * rows * tokens.size
    return whole(dispatch_kernel, [slot, tokens], [shape] * Y, flops, "dispatch")


def plane_shift(parts, sign, earlier=()):
    arrived = [shift(part, dy=sign * dy) for dy, part in enumerate(parts)]
    swapped = jnp.stack([part[1] for part in arrived])
    if earlier:
        swapped = after(swapped, *earlier)
    return [*arrived, shift(swapped, dcore=1)]


def rows_of(refs):
    return [ref.at[0] for ref in refs[:Y]] + [refs[Y].at[dy] for dy in range(Y)]


def up_kernel(*refs):
    rows, blocks = rows_of(refs), refs[Y + 1 : Y + 1 + X]
    outs, joined = refs[Y + 1 + X : -1], refs[-1]
    width = outs[0].shape[1]
    for number, block in enumerate(blocks):
        joined[:, number * width : (number + 1) * width] = block[...]
    for place, part in enumerate(rows):
        count = part.shape[0]
        product = jnp.dot(part[...], joined[...], preferred_element_type=jnp.float32)
        for number, out in enumerate(outs):
            out[place * count : (place + 1) * count, :] = product[
                :, number * width : (number + 1) * width
            ].astype(jnp.bfloat16)


def up_project(rows, blocks):
    features, width = blocks[0].shape
    count = Y * CORE * rows[0].shape[1]
    return whole(
        up_kernel,
        [*rows, *blocks],
        [jax.ShapeDtypeStruct((count, width), jnp.bfloat16)] * len(blocks),
        2 * count * features * width * len(blocks),
        "up_project",
        [pltpu.VMEM((features, len(blocks) * width), jnp.bfloat16)],
    )


def down_kernel(*refs):
    hidden, blocks, outs, joined = refs[:X], refs[X : 2 * X], refs[2 * X : -1], refs[-1]
    width = hidden[0].shape[1]
    for number, block in enumerate(blocks):
        joined[:, number * width : (number + 1) * width] = block[...]
    for place in range(Y * CORE):
        out = outs[place % Y].at[place // Y]
        count = out.shape[0]
        rows = jnp.concatenate(
            [part[place * count : (place + 1) * count, :] for part in hidden], axis=1
        )
        out[...] = lax.dot_general(
            rows, joined[...], (((1,), (1,)), ((), ())), preferred_element_type=jnp.float32
        ).astype(jnp.bfloat16)


def down_project(hidden, blocks):
    features, width = blocks[0].shape
    count = hidden[0].shape[0]
    return whole(
        down_kernel,
        [*hidden, *blocks],
        [jax.ShapeDtypeStruct((CORE, count // (Y * CORE), features), jnp.bfloat16)] * Y,
        2 * count * features * width * len(blocks),
        "down_project",
        [pltpu.VMEM((features, len(blocks) * width), jnp.bfloat16)],
    )


DIRECT, PAIRED = (0, 2, 3, 4, 6, 7), (1, 5)


def combine_kernel(slot, high, low, *refs):
    outputs, outs = rows_of(refs), refs[Y + 1 :]
    features, tokens = outs[0].shape
    total = jnp.zeros((PAIR * features, slot.shape[1]), jnp.float32)
    for place, part in enumerate(outputs):
        rows = lax.broadcasted_iota(jnp.int32, (part.shape[0], slot.shape[1]), 0)
        found = slot[place : place + 1, :] == rows
        for gate in (high, low):
            share = jnp.where(found, gate[place : place + 1, :], 0.0).astype(jnp.bfloat16)
            total += lax.dot_general(
                part[...], share, (((0,), (0,)), ((), ())), preferred_element_type=jnp.float32
            )
    parts = [
        total[
            half * features : (half + 1) * features, source * tokens : (source + 1) * tokens
        ].astype(jnp.bfloat16)
        for source in range(Z)
        for half in range(PAIR)
    ]
    for out, number in zip(outs[:-1], DIRECT):
        out[...] = parts[number]
    for place, number in enumerate(PAIRED):
        outs[-1][:, place * tokens : (place + 1) * tokens] = parts[number]


def combine(slot, high, low, outputs):
    tokens, features = slot.shape[1], outputs[0].shape[2]
    flops = 4 * slot.size * outputs[0].shape[1] * features
    sizes = [tokens // Z] * len(DIRECT) + [len(PAIRED) * tokens // Z]
    shapes = [jax.ShapeDtypeStruct((features // PAIR, size), jnp.bfloat16) for size in sizes]
    return whole(combine_kernel, [slot, high, low, *outputs], shapes, flops, "combine")


def local(tokens, routing, gate_weights, owner, weights, grads, first, second):
    expert_count = owner.shape[0]
    cut_count = lax.axis_size("cuts")
    token_count, features = tokens.shape
    top_count = routing.shape[1]
    capacity = 5 * token_count * top_count // (4 * expert_count)
    state_shape = weights.shape
    width = state_shape[3]
    me = lax.axis_index("expert")
    my_y, my_z, my_core = me // (Z * CORE), (me // CORE) % Z, me % CORE
    cut = lax.axis_index("cuts")
    my_pair, my_x = cut // X, cut % X
    plane = [(dcore, dy) for dcore in range(CORE) for dy in range(Y)]
    pieces = [
        array.reshape(expert_count, -1, width) for array in (weights, grads, first, second)
    ]
    state = adamw(*pieces, 8)
    order = jnp.arange(expert_count, dtype=jnp.int32)
    matches = routing[:, None, :] == order[None, :, None]
    gate = jnp.sum(jnp.where(matches, gate_weights[:, None, :], 0.0), axis=2)
    gate = jnp.where(jnp.any(matches, axis=2), gate, -1.0)
    high = gate.astype(jnp.bfloat16)
    low = (gate - high.astype(jnp.float32)).astype(jnp.bfloat16)
    wide = jnp.concatenate([tokens, shift(tokens, dpair=1), high, low], axis=1)
    near = [shift(wide, dz=dz) for dz in range(Z)]
    spread = exchange(state)
    near = jnp.concatenate(near, axis=0)
    gates = near[:, 2 * features :].T.astype(jnp.float32)
    gates = gates.reshape(2, Y, Z, CORE, Z * token_count)
    gates = lax.dynamic_index_in_dim(gates, my_z, axis=2, keepdims=False)
    high, low = (
        jnp.stack(
            [
                lax.dynamic_slice(
                    part, ((my_y + dy) % Y, my_core ^ dcore, 0), (1, 1, Z * token_count)
                )[0, 0]
                for dcore, dy in plane
            ]
        )
        for part in gates
    )
    near = near[:, : 2 * features]

    positions = jnp.arange(token_count, dtype=jnp.int32)
    earlier = (positions[:, None] < positions[None, :]).astype(jnp.bfloat16)
    named = (high >= 0.0).reshape(len(plane) * Z, token_count)
    slot = jnp.dot(
        named.astype(jnp.bfloat16), earlier, preferred_element_type=jnp.float32
    ).astype(jnp.int32)
    slot = slot + capacity * (jnp.arange(len(plane) * Z, dtype=jnp.int32) % Z)[:, None]
    slot = jnp.where(named, slot, -1).reshape(len(plane), Z * token_count)
    buffered = dispatch(slot, near, Z * capacity)

    by_cut = state[:, 0].reshape(2, cut_count, features, width)
    blocks = []
    for dx in range(X):
        block = jnp.concatenate(
            [
                lax.dynamic_slice_in_dim(by_cut, pair * X + (my_x + dx) % X, 1, axis=1)[:, 0]
                for pair in (my_pair, my_pair ^ 1)
            ],
            axis=1,
        )
        blocks.append(shift(block, dx=dx))

    incoming = plane_shift(buffered, 1, blocks)

    parts = up_project(incoming, [block[0] for block in blocks])
    total = sum(shift(part, dx=-dx).astype(jnp.float32) for dx, part in enumerate(parts))
    hidden = jax.nn.silu(total).astype(jnp.bfloat16)

    every = [shift(hidden, dx=dx) for dx in range(X)]

    holder = jnp.sum(order[None, :] * (owner[None, :] == order[:, None]), axis=1)
    holder = after(holder, hidden)
    arrived = exchange(jnp.take(spread, holder, axis=0, mode="clip"))

    expert_out = down_project(every, [block[1] for block in blocks])

    returned = plane_shift(expert_out, -1)

    *parts, paired = combine(slot, high, low, returned)
    part = dict(zip(DIRECT, parts))
    paired = shift(paired, dpair=1)
    here, across = jnp.split(paired.astype(jnp.float32), len(PAIRED), axis=1)
    across = (part[4].astype(jnp.float32) + across).astype(jnp.bfloat16)
    moved = [arrived[:, place].reshape(state_shape) for place in range(3)]
    mixed = here + shift(across, dz=-2).astype(jnp.float32)
    for number in (2, 3, 6, 7):
        mixed += shift(part[number], dz=-(number // PAIR), dpair=number % PAIR).astype(jnp.float32)
    mixed = (mixed + after(part[0], *moved).astype(jnp.float32)).T
    return (mixed.astype(jnp.bfloat16), *moved)


def solution(mesh):
    state = P("expert", None, None, "cuts")
    return jax.shard_map(
        local,
        mesh=mesh,
        in_specs=(
            P("expert", "cuts"),
            P("expert", None),
            P("expert", None),
            P(),
            state,
            state,
            state,
            state,
        ),
        out_specs=(P("expert", "cuts"), state, state, state),
        check_vma=False,
    )
```
